32 devices in a mesh: lat: 16 (over z, x, core), rad: 2 (over y).
Axes of the slice: x: 2, y: 2, z: 4, core: 2. Of those that a mesh axis runs over, the one named last changes fastest.
Arguments:
- fourier: bfloat16 [2, 2, 256, 2, 16, 1152], P(None, None, 'rad', None, None, 'lat'), may hold values from -6 to 6
- legendre: bfloat16 [16, 256, 1152], P('lat'), may hold values from -0.1875 to 0.1875
- inverse: bfloat16 [256, 512, 512], P('lat', 'rad'), may hold values from -0.25 to 0.25
- order_of_slot: int32 [16], replicated, may hold values from 0 to 15, each once
- degree_of_slot: int32 [256], replicated, may hold values from 0 to 255, each once
- degree_count: int32 [16], replicated, may hold values from 1 to 256, as said below
Outputs:
- solved: float32 [256, 512, 2, 16], P('lat', 'rad')
The draws below stay inside these ranges and needn't reach their ends.
Inputs may be any that keep to these rules, and one draw needn't show every extreme that they name: `order_of_slot`: a permutation; the index p of lat is given slot p. `degree_of_slot`: a permutation; the index p of lat is given slots p * 16 to (p + 1) * 16 - 1. Order k is live on the last degree_count[k] degrees of the band; some order has all 256.
All inputs are finite; a program needn't handle non-finite values.
Results may differ from the reference program's by a relative error of at most 0.0042.
Values may be sent and summed in bfloat16 or wider, within the bound.
No kernel may reach another device: no remote copies, remote signals or barrier semaphores. Data moves between devices by JAX's collectives and lax.ppermute only.
A program may use at most 64 MiB of HBM per device.

```python
import jax
import jax.numpy as jnp
from jax import lax

NH = 1152
NR = 256
M = 16
NDEG = 256


def draw_degree_count(key, part):
    drawn = jax.random.randint(key, (M,), 1, NDEG + 1)
    longest = jax.random.randint(jax.random.fold_in(key, 7), (), 0, M)
    return jnp.where(jnp.arange(M) == longest, NDEG, drawn).astype(jnp.int32)


def level_of(own_key, dims, split, least, largest):
    level = 1.0
    for dim, shards_of in split:
        draws = jax.random.uniform(jax.random.fold_in(jax.random.fold_in(own_key, 6), dim), (shards_of,), jnp.float32, least / len(split), largest / len(split))
        level = level * jnp.repeat(jnp.exp(draws), dims[dim] // shards_of).reshape((-1,) + (1,) * (len(dims) - 1 - dim))
    return level


def bell_draw(own_key, dims, width, limit, shards=(), kind=jnp.bfloat16):
    values = jax.random.normal(own_key, dims, jnp.float32) * width
    if len(shards) > 0:
        values = level_of(own_key, dims, shards, -0.22, 0.18) * values
    return jnp.clip(values, min=-limit, max=limit).astype(kind)


def setup_inputs(seed: int = 0) -> dict:
    key_list = jax.random.split(jax.random.key(seed), 7)
    return {
        "fourier": bell_draw(key_list[0], (2, 2, NR, 2, M, NH), 1.0, 6.0, ((2, 2), (5, 16))),
        "legendre": bell_draw(key_list[1], (M, NDEG, NH), NH ** -0.5, 0.1875, ((0, 16),)),
        "inverse": bell_draw(key_list[2], (NDEG, 2 * NR, 2 * NR), (2 * NR) ** -0.5, 0.25, ((0, 16), (1, 2))),
        "order_of_slot": jax.random.permutation(key_list[3], M).astype(jnp.int32),
        "degree_of_slot": jax.random.permutation(key_list[4], NDEG).astype(jnp.int32),
        "degree_count": draw_degree_count(jax.random.fold_in(key_list[6], 71), 0),
    }


def reference(fourier, legendre, inverse, order_of_slot, degree_of_slot, degree_count):
    picked = jnp.take(fourier, order_of_slot.astype(jnp.int32), axis=4)
    north_rows = picked[:, :, :, 0].astype(jnp.float32)
    south_rows = picked[:, :, :, 1].astype(jnp.float32)
    even_part = (north_rows + south_rows).astype(jnp.bfloat16)
    odd_part = (north_rows - south_rows).astype(jnp.bfloat16)
    counts = jnp.take(degree_count, order_of_slot.astype(jnp.int32))
    first_live = (NDEG - counts).astype(jnp.int32)
    band_index = jnp.arange(NDEG, dtype=jnp.int32)
    live_mask = band_index[None, :] >= first_live[:, None]
    use_even = ((band_index[None, :] - first_live[:, None]) % 2) == 0

    def one_slot(inputs):
        table, even_slot, odd_slot, live_row, even_row = inputs
        from_even = jnp.dot(table, even_slot.reshape(-1, NH).T, preferred_element_type=jnp.float32)
        from_odd = jnp.dot(table, odd_slot.reshape(-1, NH).T, preferred_element_type=jnp.float32)
        chosen = jnp.where(even_row[:, None], from_even, from_odd)
        return jnp.where(live_row[:, None], chosen, jnp.float32(0.0)).astype(jnp.bfloat16)

    coefficients = lax.map(one_slot, (legendre, jnp.moveaxis(even_part, 3, 0), jnp.moveaxis(odd_part, 3, 0), live_mask, use_even))
    regrouped = jnp.take(coefficients, degree_of_slot.astype(jnp.int32), axis=1)
    regrouped = regrouped.reshape(M, NDEG, 2, 2, NR)

    def one_degree(inputs):
        matrix, block_rows = inputs
        right_side = jnp.transpose(block_rows, (1, 3, 2, 0)).reshape(2 * NR, 2 * M)
        product = jnp.dot(matrix, right_side, preferred_element_type=jnp.float32)
        return product.reshape(2 * NR, 2, M)

    return lax.map(one_degree, (inverse, jnp.moveaxis(regrouped, 1, 0)))
```

```python
import functools

import jax
import jax.numpy as jnp
from jax import lax
from jax.experimental import pallas as pl
from jax.experimental.pallas import tpu as pltpu
from jax.sharding import PartitionSpec as P

BF16 = jnp.bfloat16
F32 = jnp.float32
PARAMS = pltpu.CompilerParams(vmem_limit_bytes=12 * 1024 * 1024)
NT = (((1,), (1,)), ((), ()))
VMEM = pl.BlockSpec(memory_space=pltpu.VMEM)
SMEM = pl.BlockSpec(memory_space=pltpu.SMEM)
MEMBERS = 4
PLANES = 4
SHELL_PARTS = 2


def struct(shape, dtype=BF16):
    return jax.ShapeDtypeStruct(shape, dtype)


def place():
    index = lax.axis_index("lat")
    return index // MEMBERS, index % MEMBERS


def call(kernel, name, in_specs, out_shape, scratch=(), **extra):
    many = isinstance(out_shape, (list, tuple))
    return pl.pallas_call(
        kernel,
        in_specs=in_specs,
        out_specs=[VMEM] * len(out_shape) if many else VMEM,
        out_shape=out_shape,
        scratch_shapes=list(scratch),
        compiler_params=PARAMS,
        name=name,
        **extra,
    )


def fold_kernel(order_ref, x_ref, *out_refs):
    _, mine = place()
    parts, rows, shells = x_ref.shape[1], x_ref.shape[4], x_ref.shape[5]
    for k in range(MEMBERS):
        for plane in range(PLANES):
            order = order_ref[plane * MEMBERS + (mine ^ k)]
            for c in range(parts):
                lanes = slice(c * shells, (c + 1) * shells)
                north = x_ref[0, c, 0, order].astype(F32)
                south = x_ref[0, c, 1, order].astype(F32)
                out_refs[k][plane, 0:rows, lanes] = (north + south).astype(BF16)
                out_refs[k][plane, rows : 2 * rows, lanes] = (north - south).astype(BF16)


def fold(x, order_of_slot, chunk):
    field, part, parts = chunk
    hemis, orders, rows, shells = x.shape[2:]
    block = pl.BlockSpec((1, parts, hemis, orders, rows, shells), lambda i: (field, part // parts, 0, 0, 0, 0))
    out = struct((PLANES, 2 * rows, parts * shells))
    return call(fold_kernel, "fold", [SMEM, block], [out] * MEMBERS, grid=(1,))(order_of_slot, x)


def turn_kernel(table_ref, *refs):
    plane, _ = place()
    out_refs, turned = refs[:-1], refs[-1]
    turned[...] = table_ref[0].T
    members, rows, _ = out_refs[0].shape
    for k in range(PLANES):
        start = pl.multiple_of((plane ^ k) * (members * rows), 16)
        window = turned[pl.ds(start, members * rows), :]
        for q in range(members):
            out_refs[k][q] = window[q * rows : (q + 1) * rows]


def turn(legendre):
    _, band, latitudes = legendre.shape
    out = struct((MEMBERS, latitudes // (MEMBERS * PLANES), band))
    return call(turn_kernel, "turn", [VMEM], [out] * PLANES, [pltpu.VMEM((latitudes, band), BF16)])(legendre)


def table_kernel(order_ref, count_ref, degree_ref, *refs):
    plane, mine = place()
    in_refs, out_ref = refs[:-1], refs[-1]
    band = in_refs[0].shape[2]
    slots = degree_ref.shape[0]
    column = lax.broadcasted_iota(jnp.int32, (slots, band), 1)
    lane = lax.broadcasted_iota(jnp.int32, (1, band), 1)
    picks = (degree_ref[...] == column).astype(F32).astype(BF16)
    for k in range(PLANES):
        first = band - count_ref[order_ref[(plane ^ k) * MEMBERS + mine]]
        live = lane >= first
        even = ((lane - first) & 1) == 0
        stack = []
        for q in range(MEMBERS):
            block = in_refs[k][mine ^ q].astype(F32)
            stack.append(jnp.where(live & even, block, 0.0))
            stack.append(jnp.where(live & ~even, block, 0.0))
        stacked = jnp.concatenate(stack, axis=0).astype(BF16)
        out_ref[plane ^ k] = lax.dot_general(picks, stacked, NT, preferred_element_type=F32).astype(BF16)


def tables(order_of_slot, degree_count, degree_column, blocks):
    members, rows, band = blocks[0].shape
    out = struct((PLANES, degree_column.shape[0], members * 2 * rows))
    return call(table_kernel, "tables", [SMEM] * 2 + [VMEM] * (1 + PLANES), out)(
        order_of_slot, degree_count, degree_column, *blocks
    )


def analyze_kernel(table_ref, *refs):
    plane, _ = place()
    in_refs, (keep_ref, send_ref, total) = refs[:MEMBERS], refs[MEMBERS:]
    share = keep_ref.shape[2]
    for s in range(PLANES):
        folds = jnp.concatenate([ref[s] for ref in in_refs], axis=0)
        total[s] = jnp.dot(table_ref[s], folds, preferred_element_type=F32)
    for k in range(PLANES // 2):
        start = pl.multiple_of((plane ^ (2 * k)) * share, 8)
        keep_ref[k] = total[:, pl.ds(start, share), :]
        start = pl.multiple_of((plane ^ (2 * k + 1)) * share, 8)
        send_ref[k] = total[:, pl.ds(start, share), :].astype(BF16)


def analyze(table, received):
    slots, width = table.shape[1], received[0].shape[2]
    half = (PLANES // 2, PLANES, slots // PLANES, width)
    return call(
        analyze_kernel,
        "analyze",
        [VMEM] * (1 + MEMBERS),
        [struct(half, F32), struct(half)],
        [pltpu.VMEM((PLANES, slots, width), F32)],
    )(table, *received)


def pair_kernel(keep_ref, got_ref, own_ref, send_ref):
    own_ref[...] = keep_ref[0] + got_ref[0].astype(F32)
    send_ref[...] = (keep_ref[1] + got_ref[1].astype(F32)).astype(BF16)


def pair(keep, got):
    return call(pair_kernel, "pair", [VMEM] * 2, [struct(keep.shape[1:], F32), struct(keep.shape[1:])])(keep, got)


def total_kernel(count, *refs):
    _, mine = place()
    outs = refs[2 * count : 4 * count]
    scratches = refs[4 * count :]
    for i in range(count):
        own_ref, got_ref, total = refs[2 * i], refs[2 * i + 1], scratches[i]
        total[...] = own_ref[...] + got_ref[...].astype(F32)
        keep_ref, send_ref = outs[2 * i], outs[2 * i + 1]
        share = keep_ref.shape[2]
        for k in range(MEMBERS // 2):
            start = pl.multiple_of((mine ^ (2 * k)) * share, 8)
            keep_ref[k] = total[:, pl.ds(start, share), :].astype(BF16)
            start = pl.multiple_of((mine ^ (2 * k + 1)) * share, 8)
            send_ref[k] = total[:, pl.ds(start, share), :].astype(BF16)


def add_up(own, got):
    planes, slots, width = own.shape
    half = struct((MEMBERS // 2, planes, slots // MEMBERS, width))
    return call(
        functools.partial(total_kernel, 1),
        "add_up",
        [VMEM] * 2,
        [half] * 2,
        [pltpu.VMEM((planes, slots, width), F32)],
    )(own, got)


def join_kernel(keep_ref, got_ref, near_ref, far_ref):
    for k, ref in enumerate((near_ref, far_ref)):
        ref[0] = keep_ref[k]
        ref[1] = got_ref[k]


def join(keep, got):
    out = struct((2,) + keep.shape[1:])
    return call(join_kernel, "join", [VMEM] * 2, [out] * 2)(keep, got)


def solve_kernel(keys, inverse_ref, *refs):
    _, mine = place()
    column = lax.axis_index("rad")
    in_refs, out_ref, rows_ref = refs[:-2], refs[-2], refs[-1]
    orders = MEMBERS * PLANES
    per_slot = in_refs[0].shape[2]
    shells = rows_ref.shape[-1]
    for ((field, part, parts), dx, dy), ref in zip(keys, in_refs, strict=True):
        for j in range(2):
            member = mine ^ (2 * dx + j)
            for s in range(PLANES):
                value = ref[j, s].astype(F32)
                for c in range(parts):
                    rows_ref[part + c, field, column ^ dy, pl.ds(s * MEMBERS + member, per_slot, stride=orders), :] = (
                        value[:, c * shells : (c + 1) * shells]
                    )
    parts, fields, columns = rows_ref.shape[:3]
    for t in range(per_slot):
        window = slice(t * orders, (t + 1) * orders)
        left = jnp.concatenate(
            [
                jnp.concatenate(
                    [rows_ref[c, f, y, window, :] for f in range(fields) for y in range(columns)], axis=1
                )
                for c in range(parts)
            ],
            axis=0,
        ).astype(BF16)
        product = lax.dot_general(left, inverse_ref[t], NT, preferred_element_type=F32)
        for c in range(parts):
            out_ref[t, c] = product[c * orders : (c + 1) * orders]


def solve(inverse, pieces, fields, parts, shells):
    degrees, rows, _ = inverse.shape
    keys = list(pieces)
    orders = MEMBERS * PLANES
    return call(
        functools.partial(solve_kernel, keys),
        "solve",
        [VMEM] * (1 + len(keys)),
        struct((degrees, parts, orders, rows), F32),
        [pltpu.VMEM((parts, fields, SHELL_PARTS, degrees * orders, shells), F32)],
    )(inverse, *[pieces[key] for key in keys])


def along_lat(value, step):
    return lax.ppermute(value, "lat", [(i, i ^ step) for i in range(MEMBERS * PLANES)])


def to_owner(value, step, dy):
    pairs = [
        (i * SHELL_PARTS + j, (i ^ step) * SHELL_PARTS + (j ^ dy))
        for i in range(MEMBERS * PLANES)
        for j in range(SHELL_PARTS)
    ]
    return lax.ppermute(value, ("lat", "rad"), pairs)


def in_steps(fourier, legendre, inverse, order_of_slot, degree_of_slot, degree_count):
    x = jnp.transpose(fourier, (0, 1, 3, 4, 5, 2))
    fields, parts, shells = x.shape[0], x.shape[1], x.shape[5]
    chunks = [(0, 0, 2), (1, 0, 1), (1, 1, 1)]
    received = {}
    packed = fold(x, order_of_slot, chunks[0])
    received[chunks[0]] = last = [packed[0]] + [along_lat(packed[k], k) for k in (1, 2, 3)]
    turned = turn(legendre)
    blocks = [turned[0]] + [along_lat(turned[k], k * MEMBERS) for k in range(1, PLANES)]
    for chunk in chunks[1:]:
        packed = fold(x, order_of_slot, chunk)
        sent = []
        for k in (1, 2, 3):
            value, last[k] = lax.optimization_barrier((packed[k], last[k]))
            sent.append(along_lat(value, k))
        received[chunk] = last = [packed[0]] + sent
    table = tables(order_of_slot, degree_count, degree_of_slot[:, None], blocks)
    pieces = {}
    for chunk in chunks:
        keep, send = analyze(table, received[chunk])
        own, send = pair(keep, along_lat(send, MEMBERS))
        keep, send = add_up(own, along_lat(send, 2 * MEMBERS))
        near, far = join(keep, along_lat(send, 1))
        pieces[chunk, 0, 0] = near
        pieces[chunk, 1, 0] = to_owner(far, 2, 0)
        pieces[chunk, 0, 1] = to_owner(near, 0, 1)
        pieces[chunk, 1, 1] = to_owner(far, 2, 1)
    solved = solve(inverse, pieces, fields, parts, shells)
    return jnp.transpose(solved, (0, 3, 1, 2))


def plain(fourier, legendre, inverse, order_of_slot, degree_of_slot, degree_count):
    slot_count, band_size = legendre.shape[:2]
    lat_index = lax.axis_index("lat")
    my_orders = lax.dynamic_slice_in_dim(order_of_slot, lat_index * slot_count, slot_count)
    first_live = band_size - jnp.take(degree_count, my_orders)
    picked = jnp.take(fourier, order_of_slot, axis=4)
    received = lax.all_to_all(picked, "lat", split_axis=4, concat_axis=5, tiled=True)
    north_rows = received[:, :, :, 0].astype(F32)
    south_rows = received[:, :, :, 1].astype(F32)
    even_part = (north_rows + south_rows).astype(BF16)
    odd_part = (north_rows - south_rows).astype(BF16)
    band_index = lax.broadcasted_iota(jnp.int32, (slot_count, band_size), 1)
    live_mask = band_index >= first_live[:, None]
    use_even = (band_index - first_live[:, None]) % 2 == 0
    full_even = jnp.einsum("ojn,fcron->ojfcr", legendre, even_part, preferred_element_type=F32)
    full_odd = jnp.einsum("ojn,fcron->ojfcr", legendre, odd_part, preferred_element_type=F32)
    chosen = jnp.where(use_even[:, :, None, None, None], full_even, full_odd)
    coefficients = jnp.where(live_mask[:, :, None, None, None], chosen, 0.0).astype(BF16)
    by_degree = jnp.take(coefficients, degree_of_slot, axis=1)
    at_owner = lax.all_to_all(by_degree, "lat", split_axis=1, concat_axis=0, tiled=True)
    degrees, rows, columns = inverse.shape
    matrices = inverse.reshape(degrees, rows, 2, columns // 2)
    gathered = lax.all_gather(at_owner, "rad", axis=4, tiled=True)
    return jnp.einsum("tqfk,mtfck->tqcm", matrices, gathered, preferred_element_type=F32)


def solution(mesh):
    in_specs = (
        P(None, None, "rad", None, None, "lat"),
        P("lat", None, None),
        P("lat", "rad", None),
        P(),
        P(),
        P(),
    )
    fits = mesh.shape["lat"] == MEMBERS * PLANES and mesh.shape["rad"] == SHELL_PARTS
    return jax.shard_map(
        in_steps if fits else plain,
        mesh=mesh,
        in_specs=in_specs,
        out_specs=P("lat", "rad", None, None),
        check_vma=False,
    )
```

```python
import functools

import jax
import jax.numpy as jnp
from jax import lax
from jax.experimental import pallas as pl
from jax.experimental.pallas import tpu as pltpu
from jax.sharding import PartitionSpec as P

BF16 = jnp.bfloat16
F32 = jnp.float32
PARAMS = pltpu.CompilerParams(vmem_limit_bytes=12 * 1024 * 1024)
NT = (((1,), (1,)), ((), ()))
VMEM = pl.BlockSpec(memory_space=pltpu.VMEM)
SMEM = pl.BlockSpec(memory_space=pltpu.SMEM)
CHUNKS = (2, 2)
UNITS = ((0, 1), (2,), (3,))
GROUPS = ((0, 1, 2),)
COSTS = {'tables': 1}
HALF = True
CFG = {'seq': ('a0', 'p0', 'a1', 'a2', 'p1', 'p2', 't0', 'j0'), 'first': 1, 'fold': 3, 'own': 1, 'ohbm': 1}
MEMBERS = 4
PLANES = 4
SHELL_PARTS = 2


def struct(shape, dtype=BF16):
    return jax.ShapeDtypeStruct(shape, dtype)


def after(value, *others):
    return lax.optimization_barrier((value, *others))[0]


def place():
    index = lax.axis_index("lat")
    return index // MEMBERS, index % MEMBERS


def call(kernel, name, in_specs, out_shape, scratch=(), **extra):
    many = isinstance(out_shape, (list, tuple))
    return pl.pallas_call(
        kernel,
        in_specs=in_specs,
        out_specs=[VMEM] * len(out_shape) if many else VMEM,
        out_shape=out_shape,
        scratch_shapes=list(scratch),
        compiler_params=PARAMS,
        name=name,
        cost_estimate=pl.CostEstimate(
            flops=int(COSTS.get(name, 1) * 10**9), bytes_accessed=10**6, transcendentals=0
        ),
        **extra,
    )


def fold_kernel(steps, order_ref, x_ref, *out_refs):
    _, mine = place()
    rows, shells = x_ref.shape[4:]
    lanes = pl.ds(pl.multiple_of(pl.program_id(0) * shells, shells), shells)
    targets = [ref.at[i] for ref in out_refs for i in range(ref.shape[0])]
    for k, out_ref in zip(steps, targets, strict=True):
        for plane in range(PLANES):
            order = order_ref[plane * MEMBERS + (mine ^ k)]
            north = x_ref[0, 0, 0, order].astype(BF16 if HALF else F32)
            south = x_ref[0, 0, 1, order].astype(BF16 if HALF else F32)
            out_ref[plane, 0:rows, lanes] = (north + south).astype(BF16)
            out_ref[plane, rows : 2 * rows, lanes] = (north - south).astype(BF16)


def fold(x, order_of_slot, blocks, steps):
    _, parts, hemis, orders, rows, shells = x.shape
    first = blocks[0][0] * parts + blocks[0][1]
    block = pl.BlockSpec(
        (1, 1, hemis, orders, rows, shells),
        lambda i: ((first + i) // parts, (first + i) % parts, 0, 0, 0, 0),
    )
    out = (PLANES, 2 * rows, len(blocks) * shells)
    if CFG.get('hbm', 1):
        x = pltpu.with_memory_space_constraint(x, pltpu.HBM)
    if CFG.get('ohbm', 0):
        order_of_slot = pltpu.with_memory_space_constraint(order_of_slot, pltpu.HBM)
    return call(
        functools.partial(fold_kernel, sum(steps, ())),
        "fold",
        [SMEM, block],
        [struct((len(group),) + out) for group in steps],
        grid=(len(blocks),),
    )(order_of_slot, x)


def pass_kernel(across_ref, got_ref, out_ref):
    out_ref[0] = across_ref[0]
    out_ref[1] = got_ref[1]


def pass_on(across, got):
    return call(pass_kernel, "pass_on", [VMEM] * 2, struct(got.shape))(across, got)


def turn_kernel(table_ref, *refs):
    plane, _ = place()
    out_refs, turned = refs[:-1], refs[-1]
    turned[...] = table_ref[0].T
    members, rows, _ = out_refs[0].shape
    for k in range(PLANES):
        start = pl.multiple_of((plane ^ k) * (members * rows), 16)
        window = turned[pl.ds(start, members * rows), :]
        for q in range(members):
            out_refs[k][q] = window[q * rows : (q + 1) * rows]


def turn(legendre):
    _, band, latitudes = legendre.shape
    out = struct((MEMBERS, latitudes // (MEMBERS * PLANES), band))
    return call(turn_kernel, "turn", [VMEM], [out] * PLANES, [pltpu.VMEM((latitudes, band), BF16)])(legendre)


def table_kernel(order_ref, count_ref, degree_ref, *refs):
    plane, mine = place()
    in_refs, out_ref = refs[:-1], refs[-1]
    band = in_refs[0].shape[2]
    slots = degree_ref.shape[0]
    column = lax.broadcasted_iota(jnp.int32, (slots, band), 1)
    lane = lax.broadcasted_iota(jnp.int32, (1, band), 1)
    picks = (degree_ref[...] == column).astype(F32).astype(BF16)
    for k in range(PLANES):
        first = band - count_ref[order_ref[(plane ^ k) * MEMBERS + mine]]
        live = lane >= first
        even = ((lane - first) & 1) == 0
        stack = []
        for q in range(MEMBERS):
            block = in_refs[k][mine ^ q].astype(F32)
            stack.append(jnp.where(live & even, block, 0.0))
            stack.append(jnp.where(live & ~even, block, 0.0))
        stacked = jnp.concatenate(stack, axis=0).astype(BF16)
        out_ref[plane ^ k] = lax.dot_general(picks, stacked, NT, preferred_element_type=F32).astype(BF16)


def tables(order_of_slot, degree_count, degree_column, blocks):
    members, rows, band = blocks[0].shape
    out = struct((PLANES, degree_column.shape[0], members * 2 * rows))
    return call(table_kernel, "tables", [SMEM] * 2 + [VMEM] * (1 + PLANES), out)(
        order_of_slot, degree_count, degree_column, *blocks
    )


def analyze_kernel(windows, table_ref, *refs):
    in_refs, (keep_ref, send_ref, total) = refs[:-3], refs[-3:]
    plane, _ = place()
    share = keep_ref.shape[2]
    lane = 0
    for i, (first, width) in enumerate(windows):
        own_ref, core_ref, across_ref = in_refs[3 * i : 3 * i + 3]
        lanes = slice(first, first + width)
        for s in range(PLANES):
            folds = jnp.concatenate(
                [own_ref[0, s, :, lanes], core_ref[0, s, :, lanes], across_ref[0, s, :, lanes], across_ref[1, s, :, lanes]],
                axis=0,
            )
            total[s, :, lane : lane + width] = jnp.dot(table_ref[s], folds, preferred_element_type=F32)
        lane += width
    for k in range(PLANES // 2):
        start = pl.multiple_of((plane ^ (2 * k)) * share, 8)
        keep_ref[k] = total[:, pl.ds(start, share), :]
        start = pl.multiple_of((plane ^ (2 * k + 1)) * share, 8)
        send_ref[k] = total[:, pl.ds(start, share), :].astype(BF16)


def analyze(table, taken):
    slots = table.shape[1]
    windows = [(first, width) for first, width, _ in taken]
    width = sum(width for _, width in windows)
    half = (PLANES // 2, PLANES, slots // PLANES, width)
    return call(
        functools.partial(analyze_kernel, windows),
        "analyze",
        [VMEM] * (1 + 3 * len(taken)),
        [struct(half, F32), struct(half)],
        [pltpu.VMEM((PLANES, slots, width), F32)],
    )(table, *[value for _, _, got in taken for value in got])


def pair_kernel(keep_ref, got_ref, own_ref, send_ref):
    own_ref[...] = keep_ref[0] + got_ref[0].astype(F32)
    send_ref[...] = (keep_ref[1] + got_ref[1].astype(F32)).astype(BF16)


def pair(keep, got):
    return call(pair_kernel, "pair", [VMEM] * 2, [struct(keep.shape[1:], F32), struct(keep.shape[1:])])(keep, got)


def total_kernel(*refs):
    _, mine = place()
    in_refs, (keep_ref, send_ref, total) = refs[:-3], refs[-3:]
    share = keep_ref.shape[2]
    lane = 0
    for own_ref, got_ref in zip(in_refs[0::2], in_refs[1::2], strict=True):
        width = own_ref.shape[2]
        total[:, :, lane : lane + width] = own_ref[...] + got_ref[...].astype(F32)
        lane += width
    for k in range(MEMBERS // 2):
        start = pl.multiple_of((mine ^ (2 * k)) * share, 8)
        keep_ref[k] = total[:, pl.ds(start, share), :].astype(BF16)
        start = pl.multiple_of((mine ^ (2 * k + 1)) * share, 8)
        send_ref[k] = total[:, pl.ds(start, share), :].astype(BF16)


def add_up(pairs):
    planes, slots, _ = pairs[0][0].shape
    width = sum(own.shape[2] for own, _ in pairs)
    half = struct((MEMBERS // 2, planes, slots // MEMBERS, width))
    return call(
        total_kernel,
        "add_up",
        [VMEM] * (2 * len(pairs)),
        [half] * 2,
        [pltpu.VMEM((planes, slots, width), F32)],
    )(*[value for two in pairs for value in two])


def join_kernel(keep_ref, got_ref, near_ref, far_ref):
    for k, ref in enumerate((near_ref, far_ref)):
        ref[0] = keep_ref[k]
        ref[1] = got_ref[k]


def join(keep, got):
    out = struct((2,) + keep.shape[1:])
    return call(join_kernel, "join", [VMEM] * 2, [out] * 2)(keep, got)


def solve_kernel(keys, step, inverse_ref, *refs):
    _, mine = place()
    column = lax.axis_index("rad") ^ step
    in_refs, (out_ref, rows_ref) = refs[: len(keys)], refs[-2:]
    orders = MEMBERS * PLANES
    per_slot = in_refs[0].shape[2]
    parts, fields, _, shells = rows_ref.shape
    for (blocks, dx, _), ref in zip(keys, in_refs, strict=True):
        for j in range(2):
            member = mine ^ (2 * dx + j)
            for s in range(PLANES):
                value = ref[j, s].astype(F32)
                for i, (field, part) in enumerate(blocks):
                    rows_ref[part, field, pl.ds(s * MEMBERS + member, per_slot, stride=orders), :] = (
                        value[:, i * shells : (i + 1) * shells]
                    )
    lanes = [pl.ds(pl.multiple_of((f * SHELL_PARTS + column) * shells, shells), shells) for f in range(fields)]
    for t in range(per_slot):
        window = slice(t * orders, (t + 1) * orders)
        left = jnp.concatenate(
            [
                jnp.concatenate([rows_ref[c, f, window, :] for f in range(fields)], axis=1)
                for c in range(parts)
            ],
            axis=0,
        ).astype(BF16)
        right = jnp.concatenate([inverse_ref[t, :, lane] for lane in lanes], axis=1)
        product = lax.dot_general(left, right, NT, preferred_element_type=F32)
        for c in range(parts):
            value = product[c * orders : (c + 1) * orders]
            if step:
                value = value + refs[len(keys)][t, c]
            out_ref[t, c] = value


def solve(inverse, pieces, fields, parts, shells):
    degrees, rows, _ = inverse.shape
    orders = MEMBERS * PLANES
    part = ()
    for step in range(SHELL_PARTS):
        keys = [key for key in pieces if key[2] == step]
        part = (
            call(
                functools.partial(solve_kernel, keys, step),
                "solve",
                [VMEM] * (1 + len(keys) + len(part)),
                struct((degrees, parts, orders, rows), F32),
                [pltpu.VMEM((parts, fields, degrees * orders, shells), F32)],
            )(inverse, *[pieces[key] for key in keys], *part),
        )
    return part[0]


def along_lat(value, step):
    return lax.ppermute(value, "lat", [(i, i ^ step) for i in range(MEMBERS * PLANES)])


def to_owner(value, step, dy):
    pairs = [
        (i * SHELL_PARTS + j, (i ^ step) * SHELL_PARTS + (j ^ dy))
        for i in range(MEMBERS * PLANES)
        for j in range(SHELL_PARTS)
    ]
    return lax.ppermute(value, ("lat", "rad"), pairs)


def in_steps(fourier, legendre, inverse, order_of_slot, degree_of_slot, degree_count):
    x = jnp.transpose(fourier, (0, 1, 3, 4, 5, 2))
    fields, parts, shells = x.shape[0], x.shape[1], x.shape[5]
    every = [(f, c) for f in range(fields) for c in range(parts)]
    chunks = [tuple(every[sum(CHUNKS[:i]) : sum(CHUNKS[: i + 1])]) for i in range(len(CHUNKS))]
    n = len(chunks)
    def dep_on(value, *others):
        return after(value, *others) if others else value
    first = CFG.get('first', 1)
    if first == 2:
        turned = turn(legendre)
        x = after(x, turned[0])
    packed = []
    got = []
    turned = None if first != 2 else turned
    def start(i, *deps):
        across, send = fold(dep_on(x, *deps), order_of_slot, chunks[i], ((2,), (1, 3)))
        core = along_lat(send, 1)
        out = pass_on(across, core)
        got.append([None, core, along_lat(out, 2)])
        return across, out
    across0, out0 = start(0)
    if first != 2:
        turned = turn(dep_on(legendre, *([across0] if first else [])))
    ls = {k: along_lat(turned[k], k * MEMBERS) for k in (2, 3, 1)}
    l1, l2, l3 = ls[1], ls[2], ls[3]
    for i in range(1, n):
        across0, out0 = start(i, {1: out0, 0: across0, 2: l1, 3: turned[0]}[CFG.get('fold', 1)])
    blocks = [turned[0], l1, l2, l3]
    dcol = degree_of_slot[:, None]
    if CFG.get('own', 1):
        first_own = fold(after(x, {1: l1, 2: got[0][2]}[CFG.get('own', 1)]), order_of_slot, chunks[0], ((0,),))[0]
        got[0][0] = first_own
        dcol = after(dcol, first_own)
    table = tables(order_of_slot, degree_count, dcol, blocks)
    last_own = [table]
    def own_of(i):
        if got[i][0] is None:
            got[i][0] = fold(dep_on(x, *last_own), order_of_slot, chunks[i], ((0,),))[0]
        return got[i]
    where = {}
    for i, chunk in enumerate(chunks):
        for j, block in enumerate(chunk):
            where[every.index(block)] = (i, j)
    keeps = {}
    pairs = {}
    joins = {}
    pieces = {}
    last = []
    for step in CFG.get('seq', ()):
        kind, i = step[0], int(step[1:])
        if kind == 'a':
            by = {}
            for block in UNITS[i]:
                ci, j = where[block]
                by.setdefault(ci, []).append(j)
            taken = [(js[0] * shells, len(js) * shells, own_of(ci)) for ci, js in by.items()]
            keep, send = analyze(dep_on(table, *last), taken)
            keeps[i] = (keep, along_lat(send, MEMBERS))
            out = keep
            last_own[:] = [keep]
        elif kind == 'p':
            keep, g = keeps[i]
            own, send = pair(dep_on(keep, *last), g)
            pairs[i] = (own, along_lat(send, 2 * MEMBERS))
            out = own
        elif kind == 't':
            taken = [pairs[j] for j in GROUPS[i]]
            taken[0] = (dep_on(taken[0][0], *last), taken[0][1])
            keep, send = add_up(taken)
            joins[i] = (keep, along_lat(send, 1))
            out = keep
        elif kind == 'j':
            keep, g = joins[i]
            near, far = join(dep_on(keep, *last), g)
            key = tuple(every[b] for j in GROUPS[i] for b in UNITS[j])
            pieces[key, 0, 0] = near
            pieces[key, 1, 0] = to_owner(far, 2, 0)
            pieces[key, 0, 1] = to_owner(near, 0, 1)
            pieces[key, 1, 1] = to_owner(far, 2, 1)
            out = near
        last = [out] if CFG.get('chain', 1) else []
    solved = solve(inverse, pieces, fields, parts, shells)
    return jnp.transpose(solved, (0, 3, 1, 2))


def plain(fourier, legendre, inverse, order_of_slot, degree_of_slot, degree_count):
    slot_count, band_size = legendre.shape[:2]
    lat_index = lax.axis_index("lat")
    my_orders = lax.dynamic_slice_in_dim(order_of_slot, lat_index * slot_count, slot_count)
    first_live = band_size - jnp.take(degree_count, my_orders)
    picked = jnp.take(fourier, order_of_slot, axis=4)
    received = lax.all_to_all(picked, "lat", split_axis=4, concat_axis=5, tiled=True)
    north_rows = received[:, :, :, 0].astype(F32)
    south_rows = received[:, :, :, 1].astype(F32)
    even_part = (north_rows + south_rows).astype(BF16)
    odd_part = (north_rows - south_rows).astype(BF16)
    band_index = lax.broadcasted_iota(jnp.int32, (slot_count, band_size), 1)
    live_mask = band_index >= first_live[:, None]
    use_even = (band_index - first_live[:, None]) % 2 == 0
    full_even = jnp.einsum("ojn,fcron->ojfcr", legendre, even_part, preferred_element_type=F32)
    full_odd = jnp.einsum("ojn,fcron->ojfcr", legendre, odd_part, preferred_element_type=F32)
    chosen = jnp.where(use_even[:, :, None, None, None], full_even, full_odd)
    coefficients = jnp.where(live_mask[:, :, None, None, None], chosen, 0.0).astype(BF16)
    by_degree = jnp.take(coefficients, degree_of_slot, axis=1)
    at_owner = lax.all_to_all(by_degree, "lat", split_axis=1, concat_axis=0, tiled=True)
    degrees, rows, columns = inverse.shape
    matrices = inverse.reshape(degrees, rows, 2, columns // 2)
    gathered = lax.all_gather(at_owner, "rad", axis=4, tiled=True)
    return jnp.einsum("tqfk,mtfck->tqcm", matrices, gathered, preferred_element_type=F32)


def solution(mesh):
    in_specs = (
        P(None, None, "rad", None, None, "lat"),
        P("lat", None, None),
        P("lat", "rad", None),
        P(),
        P(),
        P(),
    )
    fits = mesh.shape["lat"] == MEMBERS * PLANES and mesh.shape["rad"] == SHELL_PARTS
    return jax.shard_map(
        in_steps if fits else plain,
        mesh=mesh,
        in_specs=in_specs,
        out_specs=P("lat", "rad", None, None),
        check_vma=False,
    )
```

```python
import functools

import jax
import jax.numpy as jnp
from jax import lax
from jax.experimental import pallas as pl
from jax.experimental.pallas import tpu as pltpu
from jax.sharding import PartitionSpec as P

BF16 = jnp.bfloat16
F32 = jnp.float32
PARAMS = pltpu.CompilerParams(vmem_limit_bytes=12 * 1024 * 1024)
NT = (((1,), (1,)), ((), ()))
VMEM = pl.BlockSpec(memory_space=pltpu.VMEM)
SMEM = pl.BlockSpec(memory_space=pltpu.SMEM)
CHUNKS = ((0, 1), (2, 3))
UNITS = ((0, 1), (2,), (3,))
PLANE_STEPS = (0, 2, 3, 1)
MEMBERS = 4
PLANES = 4
SHELL_PARTS = 2


def struct(shape, dtype=BF16):
    return jax.ShapeDtypeStruct(shape, dtype)


def after(value, *others):
    return lax.optimization_barrier((value, *others))[0] if others else value


def place():
    index = lax.axis_index("lat")
    return index // MEMBERS, index % MEMBERS


def call(kernel, name, in_specs, out_shape, scratch=(), **extra):
    many = isinstance(out_shape, (list, tuple))
    return pl.pallas_call(
        kernel,
        in_specs=in_specs,
        out_specs=[VMEM] * len(out_shape) if many else VMEM,
        out_shape=out_shape,
        scratch_shapes=list(scratch),
        compiler_params=PARAMS,
        name=name,
        cost_estimate=pl.CostEstimate(flops=10**9, bytes_accessed=10**6, transcendentals=0),
        **extra,
    )


def fold_kernel(steps, order_ref, x_ref, *out_refs):
    _, mine = place()
    rows, shells = x_ref.shape[4:]
    lanes = pl.ds(pl.multiple_of(pl.program_id(0) * shells, shells), shells)
    targets = [ref.at[i] for ref in out_refs for i in range(ref.shape[0])]
    for k, out_ref in zip(steps, targets, strict=True):
        for plane in range(PLANES):
            order = order_ref[plane * MEMBERS + (mine ^ k)]
            north = x_ref[0, 0, 0, order]
            south = x_ref[0, 0, 1, order]
            out_ref[plane, 0:rows, lanes] = north + south
            out_ref[plane, rows : 2 * rows, lanes] = north - south


def fold(x, order_of_slot, blocks, steps):
    _, parts, hemis, orders, rows, shells = x.shape
    first = blocks[0][0] * parts + blocks[0][1]
    block = pl.BlockSpec(
        (1, 1, hemis, orders, rows, shells),
        lambda i: ((first + i) // parts, (first + i) % parts, 0, 0, 0, 0),
    )
    out = (PLANES, 2 * rows, len(blocks) * shells)
    x = pltpu.with_memory_space_constraint(x, pltpu.HBM)
    order_of_slot = pltpu.with_memory_space_constraint(order_of_slot, pltpu.HBM)
    return call(
        functools.partial(fold_kernel, sum(steps, ())),
        "fold",
        [SMEM, block],
        [struct((len(group),) + out) for group in steps],
        grid=(len(blocks),),
    )(order_of_slot, x)


def pass_kernel(across_ref, got_ref, out_ref):
    out_ref[0] = across_ref[0]
    out_ref[1] = got_ref[1]


def pass_on(across, got):
    return call(pass_kernel, "pass_on", [VMEM] * 2, struct(got.shape))(across, got)


def turn_kernel(table_ref, *refs):
    plane, _ = place()
    out_refs, turned = refs[:-1], refs[-1]
    turned[...] = table_ref[0].T
    members, rows, _ = out_refs[0].shape
    for k in range(PLANES):
        start = pl.multiple_of((plane ^ k) * (members * rows), 16)
        window = turned[pl.ds(start, members * rows), :]
        for q in range(members):
            out_refs[k][q] = window[q * rows : (q + 1) * rows]


def turn(legendre):
    _, band, latitudes = legendre.shape
    out = struct((MEMBERS, latitudes // (MEMBERS * PLANES), band))
    return call(turn_kernel, "turn", [VMEM], [out] * PLANES, [pltpu.VMEM((latitudes, band), BF16)])(legendre)


def table_kernel(order_ref, count_ref, degree_ref, *refs):
    plane, mine = place()
    in_refs, out_ref = refs[:-1], refs[-1]
    band = in_refs[0].shape[2]
    slots = degree_ref.shape[0]
    column = lax.broadcasted_iota(jnp.int32, (slots, band), 1)
    lane = lax.broadcasted_iota(jnp.int32, (1, band), 1)
    picks = (degree_ref[...] == column).astype(F32).astype(BF16)
    for k, block_ref in zip(PLANE_STEPS, in_refs, strict=True):
        first = band - count_ref[order_ref[(plane ^ k) * MEMBERS + mine]]
        live = lane >= first
        even = ((lane - first) & 1) == 0
        stack = []
        for q in range(MEMBERS):
            block = block_ref[mine ^ q].astype(F32)
            stack.append(jnp.where(live & even, block, 0.0))
            stack.append(jnp.where(live & ~even, block, 0.0))
        stacked = jnp.concatenate(stack, axis=0).astype(BF16)
        out_ref[plane ^ k] = lax.dot_general(picks, stacked, NT, preferred_element_type=F32).astype(BF16)


def tables(order_of_slot, degree_count, degree_column, blocks):
    members, rows, band = blocks[0].shape
    out = struct((PLANES, degree_column.shape[0], members * 2 * rows))
    return call(table_kernel, "tables", [SMEM] * 2 + [VMEM] * (1 + PLANES), out)(
        order_of_slot, degree_count, degree_column, *blocks
    )


def analyze_kernel(windows, table_ref, *refs):
    in_refs, (keep_ref, send_ref, total) = refs[:-3], refs[-3:]
    plane, _ = place()
    share = keep_ref.shape[2]
    lane = 0
    for i, (first, width) in enumerate(windows):
        own_ref, core_ref, across_ref = in_refs[3 * i : 3 * i + 3]
        lanes = slice(first, first + width)
        for s in range(PLANES):
            folds = jnp.concatenate(
                [own_ref[0, s, :, lanes], core_ref[0, s, :, lanes], across_ref[0, s, :, lanes], across_ref[1, s, :, lanes]],
                axis=0,
            )
            total[s, :, lane : lane + width] = jnp.dot(table_ref[s], folds, preferred_element_type=F32)
        lane += width
    for k in range(PLANES // 2):
        start = pl.multiple_of((plane ^ (2 * k)) * share, 8)
        keep_ref[k] = total[:, pl.ds(start, share), :]
        start = pl.multiple_of((plane ^ (2 * k + 1)) * share, 8)
        send_ref[k] = total[:, pl.ds(start, share), :].astype(BF16)


def analyze(table, taken):
    slots = table.shape[1]
    windows = [(first, width) for first, width, _ in taken]
    width = sum(width for _, width in windows)
    half = (PLANES // 2, PLANES, slots // PLANES, width)
    return call(
        functools.partial(analyze_kernel, windows),
        "analyze",
        [VMEM] * (1 + 3 * len(taken)),
        [struct(half, F32), struct(half)],
        [pltpu.VMEM((PLANES, slots, width), F32)],
    )(table, *[value for _, _, got in taken for value in got])


def pair_kernel(keep_ref, got_ref, own_ref, send_ref):
    own_ref[...] = keep_ref[0] + got_ref[0].astype(F32)
    send_ref[...] = (keep_ref[1] + got_ref[1].astype(F32)).astype(BF16)


def pair(keep, got):
    return call(pair_kernel, "pair", [VMEM] * 2, [struct(keep.shape[1:], F32), struct(keep.shape[1:])])(keep, got)


def total_kernel(*refs):
    _, mine = place()
    in_refs, (keep_ref, send_ref, total) = refs[:-3], refs[-3:]
    share = keep_ref.shape[2]
    lane = 0
    for own_ref, got_ref in zip(in_refs[0::2], in_refs[1::2], strict=True):
        width = own_ref.shape[2]
        total[:, :, lane : lane + width] = own_ref[...] + got_ref[...].astype(F32)
        lane += width
    for k in range(MEMBERS // 2):
        start = pl.multiple_of((mine ^ (2 * k)) * share, 8)
        keep_ref[k] = total[:, pl.ds(start, share), :].astype(BF16)
        start = pl.multiple_of((mine ^ (2 * k + 1)) * share, 8)
        send_ref[k] = total[:, pl.ds(start, share), :].astype(BF16)


def add_up(pairs):
    planes, slots, _ = pairs[0][0].shape
    width = sum(own.shape[2] for own, _ in pairs)
    half = struct((MEMBERS // 2, planes, slots // MEMBERS, width))
    return call(
        total_kernel,
        "add_up",
        [VMEM] * (2 * len(pairs)),
        [half] * 2,
        [pltpu.VMEM((planes, slots, width), F32)],
    )(*[value for two in pairs for value in two])


def join_kernel(keep_ref, got_ref, near_ref, far_ref):
    for k, ref in enumerate((near_ref, far_ref)):
        ref[0] = keep_ref[k]
        ref[1] = got_ref[k]


def join(keep, got):
    out = struct((2,) + keep.shape[1:])
    return call(join_kernel, "join", [VMEM] * 2, [out] * 2)(keep, got)


def solve_kernel(keys, step, inverse_ref, *refs):
    _, mine = place()
    column = lax.axis_index("rad") ^ step
    in_refs, (out_ref, rows_ref) = refs[: len(keys)], refs[-2:]
    orders = MEMBERS * PLANES
    per_slot = in_refs[0].shape[2]
    parts, fields, _, shells = rows_ref.shape
    for (blocks, dx, _), ref in zip(keys, in_refs, strict=True):
        for j in range(2):
            member = mine ^ (2 * dx + j)
            for s in range(PLANES):
                value = ref[j, s].astype(F32)
                for i, (field, part) in enumerate(blocks):
                    rows_ref[part, field, pl.ds(s * MEMBERS + member, per_slot, stride=orders), :] = (
                        value[:, i * shells : (i + 1) * shells]
                    )
    lanes = [pl.ds(pl.multiple_of((f * SHELL_PARTS + column) * shells, shells), shells) for f in range(fields)]
    for t in range(per_slot):
        window = slice(t * orders, (t + 1) * orders)
        left = jnp.concatenate(
            [
                jnp.concatenate([rows_ref[c, f, window, :] for f in range(fields)], axis=1)
                for c in range(parts)
            ],
            axis=0,
        ).astype(BF16)
        right = jnp.concatenate([inverse_ref[t, :, lane] for lane in lanes], axis=1)
        product = lax.dot_general(left, right, NT, preferred_element_type=F32)
        for c in range(parts):
            value = product[c * orders : (c + 1) * orders]
            if step:
                value = value + refs[len(keys)][t, c]
            out_ref[t, c] = value


def solve(inverse, pieces, fields, parts, shells):
    degrees, rows, _ = inverse.shape
    orders = MEMBERS * PLANES
    part = ()
    for step in range(SHELL_PARTS):
        keys = [key for key in pieces if key[2] == step]
        part = (
            call(
                functools.partial(solve_kernel, keys, step),
                "solve",
                [VMEM] * (1 + len(keys) + len(part)),
                struct((degrees, parts, orders, rows), F32),
                [pltpu.VMEM((parts, fields, degrees * orders, shells), F32)],
            )(inverse, *[pieces[key] for key in keys], *part),
        )
    return part[0]


def along_lat(value, step):
    return lax.ppermute(value, "lat", [(i, i ^ step) for i in range(MEMBERS * PLANES)])


def to_owner(value, step, dy):
    pairs = [
        (i * SHELL_PARTS + j, (i ^ step) * SHELL_PARTS + (j ^ dy))
        for i in range(MEMBERS * PLANES)
        for j in range(SHELL_PARTS)
    ]
    return lax.ppermute(value, ("lat", "rad"), pairs)


def in_steps(fourier, legendre, inverse, order_of_slot, degree_of_slot, degree_count):
    x = jnp.transpose(fourier, (0, 1, 3, 4, 5, 2))
    fields, parts, shells = x.shape[0], x.shape[1], x.shape[5]
    every = [(f, c) for f in range(fields) for c in range(parts)]
    chunks = [tuple(every[i] for i in chunk) for chunk in CHUNKS]

    def across_x(chunk, *before):
        across, send = fold(after(x, *before), order_of_slot, chunk, ((2,), (1, 3)))
        core = along_lat(send, 1)
        return across, core, along_lat(pass_on(across, core), 2)

    def own(chunk, *before):
        return fold(after(x, *before), order_of_slot, chunk, ((0,),))[0]

    across, core0, far0 = across_x(chunks[0])
    turned = turn(after(legendre, across))
    blocks = [along_lat(turned[k], k * MEMBERS) if k else turned[0] for k in PLANE_STEPS]
    _, core1, far1 = across_x(chunks[1], turned[0])
    own0 = own(chunks[0], blocks[PLANE_STEPS.index(1)])
    table = tables(order_of_slot, degree_count, after(degree_of_slot[:, None], own0), blocks)

    def plane_step(table, first, width, got):
        keep, send = analyze(table, [(first * shells, width * shells, got)])
        return keep, along_lat(send, MEMBERS)

    def pair_step(keep, got):
        own, send = pair(keep, got)
        return own, along_lat(send, 2 * MEMBERS)

    keep0, got0 = plane_step(table, 0, 2, (own0, core0, far0))
    own1 = own(chunks[1], keep0)
    sum0 = pair_step(keep0, got0)
    keep1, got1 = plane_step(after(table, sum0[0]), 0, 1, (own1, core1, far1))
    keep2, got2 = plane_step(after(table, keep1), 1, 1, (own1, core1, far1))
    sum1 = pair_step(after(keep1, keep2), got1)
    sum2 = pair_step(after(keep2, sum1[0]), got2)
    keep, send = add_up([(after(sum0[0], sum2[0]), sum0[1]), sum1, sum2])
    near, far = join(keep, along_lat(send, 1))
    key = tuple(every[i] for unit in UNITS for i in unit)
    pieces = {
        (key, 0, 0): near,
        (key, 1, 0): to_owner(far, 2, 0),
        (key, 0, 1): to_owner(near, 0, 1),
        (key, 1, 1): to_owner(far, 2, 1),
    }
    solved = solve(inverse, pieces, fields, parts, shells)
    return jnp.transpose(solved, (0, 3, 1, 2))


def plain(fourier, legendre, inverse, order_of_slot, degree_of_slot, degree_count):
    slot_count, band_size = legendre.shape[:2]
    lat_index = lax.axis_index("lat")
    my_orders = lax.dynamic_slice_in_dim(order_of_slot, lat_index * slot_count, slot_count)
    first_live = band_size - jnp.take(degree_count, my_orders)
    picked = jnp.take(fourier, order_of_slot, axis=4)
    received = lax.all_to_all(picked, "lat", split_axis=4, concat_axis=5, tiled=True)
    north_rows = received[:, :, :, 0].astype(F32)
    south_rows = received[:, :, :, 1].astype(F32)
    even_part = (north_rows + south_rows).astype(BF16)
    odd_part = (north_rows - south_rows).astype(BF16)
    band_index = lax.broadcasted_iota(jnp.int32, (slot_count, band_size), 1)
    live_mask = band_index >= first_live[:, None]
    use_even = (band_index - first_live[:, None]) % 2 == 0
    full_even = jnp.einsum("ojn,fcron->ojfcr", legendre, even_part, preferred_element_type=F32)
    full_odd = jnp.einsum("ojn,fcron->ojfcr", legendre, odd_part, preferred_element_type=F32)
    chosen = jnp.where(use_even[:, :, None, None, None], full_even, full_odd)
    coefficients = jnp.where(live_mask[:, :, None, None, None], chosen, 0.0).astype(BF16)
    by_degree = jnp.take(coefficients, degree_of_slot, axis=1)
    at_owner = lax.all_to_all(by_degree, "lat", split_axis=1, concat_axis=0, tiled=True)
    degrees, rows, columns = inverse.shape
    matrices = inverse.reshape(degrees, rows, 2, columns // 2)
    gathered = lax.all_gather(at_owner, "rad", axis=4, tiled=True)
    return jnp.einsum("tqfk,mtfck->tqcm", matrices, gathered, preferred_element_type=F32)


def solution(mesh):
    in_specs = (
        P(None, None, "rad", None, None, "lat"),
        P("lat", None, None),
        P("lat", "rad", None),
        P(),
        P(),
        P(),
    )
    fits = mesh.shape["lat"] == MEMBERS * PLANES and mesh.shape["rad"] == SHELL_PARTS
    return jax.shard_map(
        in_steps if fits else plain,
        mesh=mesh,
        in_specs=in_specs,
        out_specs=P("lat", "rad", None, None),
        check_vma=False,
    )
```

```python
import functools

import jax
import jax.numpy as jnp
from jax import lax
from jax.experimental import pallas as pl
from jax.experimental.pallas import tpu as pltpu
from jax.sharding import PartitionSpec as P

BF16 = jnp.bfloat16
F32 = jnp.float32
PARAMS = pltpu.CompilerParams(vmem_limit_bytes=12 * 1024 * 1024)
NT = (((1,), (1,)), ((), ()))
VMEM = pl.BlockSpec(memory_space=pltpu.VMEM)
SMEM = pl.BlockSpec(memory_space=pltpu.SMEM)
CHUNKS = ((0, 1), (2, 3))
UNITS = ((0, 1), (2,), (3,))
PLANE_STEPS = (0, 2, 3, 1)
MEMBERS = 4
PLANES = 4
SHELL_PARTS = 2


def struct(shape, dtype=BF16):
    return jax.ShapeDtypeStruct(shape, dtype)


def after(value, *others):
    return lax.optimization_barrier((value, *others))[0] if others else value


def place():
    index = lax.axis_index("lat")
    return index // MEMBERS, index % MEMBERS


def call(kernel, name, in_specs, out_shape, scratch=(), **extra):
    many = isinstance(out_shape, (list, tuple))
    return pl.pallas_call(
        kernel,
        in_specs=in_specs,
        out_specs=[VMEM] * len(out_shape) if many else VMEM,
        out_shape=out_shape,
        scratch_shapes=list(scratch),
        compiler_params=PARAMS,
        name=name,
        cost_estimate=pl.CostEstimate(flops=0 if name == "solve" else 10**9, bytes_accessed=0 if name == "solve" else 10**6, transcendentals=0),
        **extra,
    )


def fold_kernel(steps, order_ref, x_ref, *out_refs):
    _, mine = place()
    rows, shells = x_ref.shape[4:]
    lanes = pl.ds(pl.multiple_of(pl.program_id(0) * shells, shells), shells)
    targets = [ref.at[i] for ref in out_refs for i in range(ref.shape[0])]
    for k, out_ref in zip(steps, targets, strict=True):
        for plane in range(PLANES):
            order = order_ref[plane * MEMBERS + (mine ^ k)]
            north = x_ref[0, 0, 0, order]
            south = x_ref[0, 0, 1, order]
            out_ref[plane, 0:rows, lanes] = north + south
            out_ref[plane, rows : 2 * rows, lanes] = north - south


def fold(x, order_of_slot, blocks, steps):
    _, parts, hemis, orders, rows, shells = x.shape
    first = blocks[0][0] * parts + blocks[0][1]
    block = pl.BlockSpec(
        (1, 1, hemis, orders, rows, shells),
        lambda i: ((first + i) // parts, (first + i) % parts, 0, 0, 0, 0),
    )
    out = (PLANES, 2 * rows, len(blocks) * shells)
    x = pltpu.with_memory_space_constraint(x, pltpu.HBM)
    order_of_slot = pltpu.with_memory_space_constraint(order_of_slot, pltpu.HBM)
    return call(
        functools.partial(fold_kernel, sum(steps, ())),
        "fold",
        [SMEM, block],
        [struct((len(group),) + out) for group in steps],
        grid=(len(blocks),),
    )(order_of_slot, x)


def pass_kernel(across_ref, got_ref, out_ref):
    out_ref[0] = across_ref[0]
    out_ref[1] = got_ref[1]


def pass_on(across, got):
    return call(pass_kernel, "pass_on", [VMEM] * 2, struct(got.shape))(across, got)


def turn_kernel(table_ref, *refs):
    plane, _ = place()
    out_refs, turned = refs[:-1], refs[-1]
    turned[...] = table_ref[0].T
    members, rows, _ = out_refs[0].shape
    for k in range(PLANES):
        start = pl.multiple_of((plane ^ k) * (members * rows), 16)
        window = turned[pl.ds(start, members * rows), :]
        for q in range(members):
            out_refs[k][q] = window[q * rows : (q + 1) * rows]


def turn(legendre):
    _, band, latitudes = legendre.shape
    out = struct((MEMBERS, latitudes // (MEMBERS * PLANES), band))
    return call(turn_kernel, "turn", [VMEM], [out] * PLANES, [pltpu.VMEM((latitudes, band), BF16)])(legendre)


def table_kernel(order_ref, count_ref, degree_ref, *refs):
    plane, mine = place()
    in_refs, out_ref = refs[:-1], refs[-1]
    band = in_refs[0].shape[2]
    slots = degree_ref.shape[0]
    column = lax.broadcasted_iota(jnp.int32, (slots, band), 1)
    lane = lax.broadcasted_iota(jnp.int32, (1, band), 1)
    picks = (degree_ref[...] == column).astype(F32).astype(BF16)
    for k, block_ref in zip(PLANE_STEPS, in_refs, strict=True):
        first = band - count_ref[order_ref[(plane ^ k) * MEMBERS + mine]]
        live = lane >= first
        even = ((lane - first) & 1) == 0
        stack = []
        for q in range(MEMBERS):
            block = block_ref[mine ^ q].astype(F32)
            stack.append(jnp.where(live & even, block, 0.0))
            stack.append(jnp.where(live & ~even, block, 0.0))
        stacked = jnp.concatenate(stack, axis=0).astype(BF16)
        out_ref[plane ^ k] = lax.dot_general(picks, stacked, NT, preferred_element_type=F32).astype(BF16)


def tables(order_of_slot, degree_count, degree_column, blocks):
    members, rows, band = blocks[0].shape
    out = struct((PLANES, degree_column.shape[0], members * 2 * rows))
    return call(table_kernel, "tables", [SMEM] * 2 + [VMEM] * (1 + PLANES), out)(
        order_of_slot, degree_count, degree_column, *blocks
    )


def analyze_kernel(windows, table_ref, *refs):
    in_refs, (keep_ref, send_ref, total) = refs[:-3], refs[-3:]
    plane, _ = place()
    share = keep_ref.shape[2]
    lane = 0
    for i, (first, width) in enumerate(windows):
        own_ref, core_ref, across_ref = in_refs[3 * i : 3 * i + 3]
        lanes = slice(first, first + width)
        for s in range(PLANES):
            folds = jnp.concatenate(
                [own_ref[0, s, :, lanes], core_ref[0, s, :, lanes], across_ref[0, s, :, lanes], across_ref[1, s, :, lanes]],
                axis=0,
            )
            total[s, :, lane : lane + width] = jnp.dot(table_ref[s], folds, preferred_element_type=F32)
        lane += width
    for k in range(PLANES // 2):
        start = pl.multiple_of((plane ^ (2 * k)) * share, 8)
        keep_ref[k] = total[:, pl.ds(start, share), :]
        start = pl.multiple_of((plane ^ (2 * k + 1)) * share, 8)
        send_ref[k] = total[:, pl.ds(start, share), :].astype(BF16)


def analyze(table, taken):
    slots = table.shape[1]
    windows = [(first, width) for first, width, _ in taken]
    width = sum(width for _, width in windows)
    half = (PLANES // 2, PLANES, slots // PLANES, width)
    return call(
        functools.partial(analyze_kernel, windows),
        "analyze",
        [VMEM] * (1 + 3 * len(taken)),
        [struct(half, F32), struct(half)],
        [pltpu.VMEM((PLANES, slots, width), F32)],
    )(table, *[value for _, _, got in taken for value in got])


def pair_kernel(keep_ref, got_ref, own_ref, send_ref):
    own_ref[...] = keep_ref[0] + got_ref[0].astype(F32)
    send_ref[...] = (keep_ref[1] + got_ref[1].astype(F32)).astype(BF16)


def pair(keep, got):
    return call(pair_kernel, "pair", [VMEM] * 2, [struct(keep.shape[1:], F32), struct(keep.shape[1:])])(keep, got)


def total_kernel(*refs):
    _, mine = place()
    in_refs, (keep_ref, send_ref, total) = refs[:-3], refs[-3:]
    share = keep_ref.shape[2]
    lane = 0
    for own_ref, got_ref in zip(in_refs[0::2], in_refs[1::2], strict=True):
        width = own_ref.shape[2]
        total[:, :, lane : lane + width] = own_ref[...] + got_ref[...].astype(F32)
        lane += width
    for k in range(MEMBERS // 2):
        start = pl.multiple_of((mine ^ (2 * k)) * share, 8)
        keep_ref[k] = total[:, pl.ds(start, share), :].astype(BF16)
        start = pl.multiple_of((mine ^ (2 * k + 1)) * share, 8)
        send_ref[k] = total[:, pl.ds(start, share), :].astype(BF16)


def add_up(pairs):
    planes, slots, _ = pairs[0][0].shape
    width = sum(own.shape[2] for own, _ in pairs)
    half = struct((MEMBERS // 2, planes, slots // MEMBERS, width))
    return call(
        total_kernel,
        "add_up",
        [VMEM] * (2 * len(pairs)),
        [half] * 2,
        [pltpu.VMEM((planes, slots, width), F32)],
    )(*[value for two in pairs for value in two])


def join_kernel(keep_ref, got_ref, near_ref, far_ref):
    for k, ref in enumerate((near_ref, far_ref)):
        ref[0] = keep_ref[k]
        ref[1] = got_ref[k]


def join(keep, got):
    out = struct((2,) + keep.shape[1:])
    return call(join_kernel, "join", [VMEM] * 2, [out] * 2)(keep, got)


def solve_kernel(keys, step, inverse_ref, *refs):
    _, mine = place()
    column = lax.axis_index("rad") ^ step
    in_refs, (out_ref, rows_ref) = refs[: len(keys)], refs[-2:]
    orders = MEMBERS * PLANES
    per_slot = in_refs[0].shape[2]
    parts, fields, _, shells = rows_ref.shape
    for (blocks, dx, _), ref in zip(keys, in_refs, strict=True):
        for j in range(2):
            member = mine ^ (2 * dx + j)
            for s in range(PLANES):
                value = ref[j, s].astype(F32)
                for i, (field, part) in enumerate(blocks):
                    rows_ref[part, field, pl.ds(s * MEMBERS + member, per_slot, stride=orders), :] = (
                        value[:, i * shells : (i + 1) * shells]
                    )
    lanes = [pl.ds(pl.multiple_of((f * SHELL_PARTS + column) * shells, shells), shells) for f in range(fields)]
    for t in range(per_slot):
        window = slice(t * orders, (t + 1) * orders)
        left = jnp.concatenate(
            [
                jnp.concatenate([rows_ref[c, f, window, :] for f in range(fields)], axis=1)
                for c in range(parts)
            ],
            axis=0,
        ).astype(BF16)
        right = jnp.concatenate([inverse_ref[t, :, lane] for lane in lanes], axis=1)
        product = lax.dot_general(left, right, NT, preferred_element_type=F32)
        for c in range(parts):
            value = product[c * orders : (c + 1) * orders]
            if step:
                value = value + refs[len(keys)][t, c]
            out_ref[t, c] = value


def solve(inverse, pieces, fields, parts, shells):
    degrees, rows, _ = inverse.shape
    orders = MEMBERS * PLANES
    part = ()
    for step in range(SHELL_PARTS):
        keys = [key for key in pieces if key[2] == step]
        part = (
            call(
                functools.partial(solve_kernel, keys, step),
                "solve",
                [VMEM] * (1 + len(keys) + len(part)),
                struct((degrees, parts, orders, rows), F32),
                [pltpu.VMEM((parts, fields, degrees * orders, shells), F32)],
            )(inverse, *[pieces[key] for key in keys], *part),
        )
    return part[0]


def along_lat(value, step):
    return lax.ppermute(value, "lat", [(i, i ^ step) for i in range(MEMBERS * PLANES)])


def to_owner(value, step, dy):
    pairs = [
        (i * SHELL_PARTS + j, (i ^ step) * SHELL_PARTS + (j ^ dy))
        for i in range(MEMBERS * PLANES)
        for j in range(SHELL_PARTS)
    ]
    return lax.ppermute(value, ("lat", "rad"), pairs)


def in_steps(fourier, legendre, inverse, order_of_slot, degree_of_slot, degree_count):
    x = jnp.transpose(fourier, (0, 1, 3, 4, 5, 2))
    fields, parts, shells = x.shape[0], x.shape[1], x.shape[5]
    every = [(f, c) for f in range(fields) for c in range(parts)]
    chunks = [tuple(every[i] for i in chunk) for chunk in CHUNKS]

    def across_x(chunk, *before):
        across, send = fold(after(x, *before), order_of_slot, chunk, ((2,), (1, 3)))
        core = along_lat(send, 1)
        return across, core, along_lat(pass_on(across, core), 2)

    def own(chunk, *before):
        return fold(after(x, *before), order_of_slot, chunk, ((0,),))[0]

    across, core0, far0 = across_x(chunks[0])
    turned = turn(after(legendre, across))
    blocks = [along_lat(turned[k], k * MEMBERS) if k else turned[0] for k in PLANE_STEPS]
    _, core1, far1 = across_x(chunks[1], turned[0])
    own0 = own(chunks[0], blocks[PLANE_STEPS.index(1)])
    table = tables(order_of_slot, degree_count, after(degree_of_slot[:, None], own0), blocks)

    def plane_step(table, first, width, got):
        keep, send = analyze(table, [(first * shells, width * shells, got)])
        return keep, along_lat(send, MEMBERS)

    def pair_step(keep, got):
        own, send = pair(keep, got)
        return own, along_lat(send, 2 * MEMBERS)

    keep0, got0 = plane_step(table, 0, 2, (own0, core0, far0))
    own1 = own(chunks[1], keep0)
    sum0 = pair_step(keep0, got0)
    keep1, got1 = plane_step(after(table, sum0[0]), 0, 1, (own1, core1, far1))
    keep2, got2 = plane_step(after(table, keep1), 1, 1, (own1, core1, far1))
    sum1 = pair_step(after(keep1, keep2), got1)
    sum2 = pair_step(after(keep2, sum1[0]), got2)
    keep, send = add_up([(after(sum0[0], sum2[0]), sum0[1]), sum1, sum2])
    near, far = join(keep, along_lat(send, 1))
    key = tuple(every[i] for unit in UNITS for i in unit)
    pieces = {
        (key, 0, 0): near,
        (key, 1, 0): to_owner(far, 2, 0),
        (key, 0, 1): to_owner(near, 0, 1),
        (key, 1, 1): to_owner(far, 2, 1),
    }
    solved = solve(inverse, pieces, fields, parts, shells)
    return jnp.transpose(solved, (0, 3, 1, 2))


def plain(fourier, legendre, inverse, order_of_slot, degree_of_slot, degree_count):
    slot_count, band_size = legendre.shape[:2]
    lat_index = lax.axis_index("lat")
    my_orders = lax.dynamic_slice_in_dim(order_of_slot, lat_index * slot_count, slot_count)
    first_live = band_size - jnp.take(degree_count, my_orders)
    picked = jnp.take(fourier, order_of_slot, axis=4)
    received = lax.all_to_all(picked, "lat", split_axis=4, concat_axis=5, tiled=True)
    north_rows = received[:, :, :, 0].astype(F32)
    south_rows = received[:, :, :, 1].astype(F32)
    even_part = (north_rows + south_rows).astype(BF16)
    odd_part = (north_rows - south_rows).astype(BF16)
    band_index = lax.broadcasted_iota(jnp.int32, (slot_count, band_size), 1)
    live_mask = band_index >= first_live[:, None]
    use_even = (band_index - first_live[:, None]) % 2 == 0
    full_even = jnp.einsum("ojn,fcron->ojfcr", legendre, even_part, preferred_element_type=F32)
    full_odd = jnp.einsum("ojn,fcron->ojfcr", legendre, odd_part, preferred_element_type=F32)
    chosen = jnp.where(use_even[:, :, None, None, None], full_even, full_odd)
    coefficients = jnp.where(live_mask[:, :, None, None, None], chosen, 0.0).astype(BF16)
    by_degree = jnp.take(coefficients, degree_of_slot, axis=1)
    at_owner = lax.all_to_all(by_degree, "lat", split_axis=1, concat_axis=0, tiled=True)
    degrees, rows, columns = inverse.shape
    matrices = inverse.reshape(degrees, rows, 2, columns // 2)
    gathered = lax.all_gather(at_owner, "rad", axis=4, tiled=True)
    return jnp.einsum("tqfk,mtfck->tqcm", matrices, gathered, preferred_element_type=F32)


def solution(mesh):
    in_specs = (
        P(None, None, "rad", None, None, "lat"),
        P("lat", None, None),
        P("lat", "rad", None),
        P(),
        P(),
        P(),
    )
    fits = mesh.shape["lat"] == MEMBERS * PLANES and mesh.shape["rad"] == SHELL_PARTS
    return jax.shard_map(
        in_steps if fits else plain,
        mesh=mesh,
        in_specs=in_specs,
        out_specs=P("lat", "rad", None, None),
        check_vma=False,
    )
```
